256 devices in a mesh: dp: 32 (over y, z_hi, core), tensor: 8 (over z_lo, x).
Axes of the slice: x: 4, y: 4, z: 8 (z_hi: 4, z_lo: 2; z = z_hi * 2 + z_lo), core: 2. Of those that a mesh axis runs over, the one named last changes fastest.
Arguments:
- cotangent: bfloat16 [32768, 4096], P(('dp', 'tensor')), may hold values from -24 to 24
- features: bfloat16 [32768, 1024], P(('dp', 'tensor')), may hold values from -24 to 24
- normed: bfloat16 [32768, 1024], P(('dp', 'tensor')), may hold values from -24 to 24
- pre_hidden: bfloat16 [32768, 4096], P('dp', 'tensor'), may hold values from -6 to 6
- pre_inner: bfloat16 [32768, 4096], P('dp', 'tensor'), may hold values from -8 to 8
- w_first: bfloat16 [1024, 4096], P(None, 'tensor'), may hold values from -0.1875 to 0.1875
- w_second: bfloat16 [4096, 4096], P('tensor'), may hold values from -0.09375 to 0.09375
- w_down: bfloat16 [4096, 1024], P('tensor'), may hold values from -0.09375 to 0.09375
Outputs:
- grad_second: float32 [4096, 4096], P('tensor', 'dp')
- grad_first: float32 [1024, 4096], P('dp', 'tensor')
- grad_down: float32 [4096, 1024], P('tensor', 'dp')
- grad_up: float32 [1024, 4096], P('dp', 'tensor')
- encoder_cotangent: bfloat16 [32768, 1024], P(('dp', 'tensor'))
The draws below stay inside these ranges and needn't reach their ends.
All inputs are finite; a program needn't handle non-finite values.
Results may differ from the reference program's by a relative error of at most 0.02.
Values may be sent and summed in bfloat16 or wider, within the bound.
A program may use at most 128 MiB of HBM per device.

```python
import math
import jax
import jax.numpy as jnp
from jax import lax

D = 1024
F = 4096
H = 4096
E = 4096
TOKENS = 32768
N_TENSOR = 8


def raised(entries, own_key, source, target, shards_of, factor):
    def block_of(position):
        return (jnp.arange(entries.shape[position]) // (entries.shape[position] // shards_of)).reshape((-1,) + (1,) * (entries.ndim - 1 - position))

    one_side = jax.random.permutation(own_key, shards_of)[block_of(target)]
    other_side = (block_of(target) + shards_of // 2) % shards_of
    return jnp.where((block_of(source) == one_side) | (block_of(source) == other_side), factor * entries, entries)


def steps_of(own_key, dims, shards, smallest, top_value):
    def one(position, parts):
        draws = jax.random.uniform(jax.random.fold_in(jax.random.fold_in(own_key, 6), position), (parts,), jnp.float32, smallest / len(shards), top_value / len(shards))
        return jnp.repeat(jnp.exp(draws), dims[position] // parts).reshape((-1,) + (1,) * (len(dims) - position - 1))

    factor_of = one(*shards[0])
    for cut in shards[1:]:
        factor_of = factor_of * one(*cut)
    return factor_of


def gaussian(rng, shape, spread, limit, cuts=(), held_as=jnp.bfloat16):
    entries = spread * jax.random.normal(rng, shape, jnp.float32)
    if cuts:
        entries = entries * steps_of(rng, shape, cuts, -0.22, 0.18)
    return jnp.clip(entries, -limit, limit).astype(held_as)


def noise_with(own_key, shape, scale, limit, shards, heavy, kind=jnp.bfloat16):
    drawn = scale * jax.random.normal(own_key, shape, jnp.float32)
    if shards:
        drawn = drawn * steps_of(own_key, shape, shards, -0.22, 0.18)
    return jnp.clip(raised(drawn, jax.random.fold_in(own_key, 3), *heavy), -limit, limit).astype(kind)


def setup_inputs(seed: int = 0) -> dict:
    splits = jax.random.split(jax.random.key(seed), 9)
    return {
        "cotangent": noise_with(splits[0], (TOKENS, E), 1.0, 24.0, ((0, 256),), (0, 1, 256, 6.0)),
        "features": noise_with(splits[1], (TOKENS, D), 1.0, 24.0, ((0, 256),), (0, 1, 256, 6.0)),
        "normed": noise_with(splits[2], (TOKENS, D), 1.0, 24.0, ((0, 256),), (0, 1, 256, 6.0)),
        "pre_hidden": gaussian(splits[3], (TOKENS, H), 1.0, 6.0, ((0, 32), (1, 8))),
        "pre_inner": gaussian(splits[4], (TOKENS, F), 1.5, 8.0, ((0, 32), (1, 8))),
        "w_first": gaussian(splits[5], (D, H), D ** -0.5, 0.1875, ((1, 8),)),
        "w_second": gaussian(splits[6], (H, E), H ** -0.5, 0.09375, ((0, 8),)),
        "w_down": gaussian(splits[7], (F, D), F ** -0.5, 0.09375, ((0, 8),)),
    }


def normal_cdf(value):
    return 0.5 * (1.0 + jax.scipy.special.erf(value * (1.0 / math.sqrt(2.0))))

def normal_pdf(value):
    return jnp.exp(-0.5 * value * value) * (1.0 / math.sqrt(2.0 * math.pi))

def reference(cotangent, features, normed, pre_hidden, pre_inner, w_first, w_second, w_down):
    factor = 1.0 / math.sqrt(TOKENS)
    pre_value = pre_hidden.astype(jnp.float32)
    hidden_act = (pre_value * normal_cdf(pre_value)).astype(jnp.bfloat16)
    d_hidden = jnp.dot(cotangent, w_second.T, preferred_element_type=jnp.float32)
    slope = normal_cdf(pre_value) + pre_value * normal_pdf(pre_value)
    d_pre = (d_hidden * slope).astype(jnp.bfloat16)
    grad_second = jnp.dot(hidden_act.T, cotangent, preferred_element_type=jnp.float32) * factor
    grad_first = jnp.dot(features.T, d_pre, preferred_element_type=jnp.float32) * factor
    width = H // N_TENSOR

    def add_block(total, index):
        start = (index * width).astype(jnp.int32)
        rows = lax.dynamic_slice_in_dim(d_pre, start, width, 1)
        weights = lax.dynamic_slice_in_dim(w_first, start, width, 1)
        partial_sum = jnp.dot(rows, weights.T, preferred_element_type=jnp.float32).astype(jnp.bfloat16)
        partial_sum = lax.optimization_barrier(partial_sum)
        return (total + partial_sum.astype(jnp.float32), None)
    start_total = jnp.zeros((TOKENS, D), jnp.float32)
    summed, _ = lax.scan(add_block, start_total, jnp.arange(N_TENSOR, dtype=jnp.int32))
    encoder_cotangent = summed.astype(jnp.bfloat16)
    inner_value = pre_inner.astype(jnp.float32)
    sig = jax.nn.sigmoid(1.702 * inner_value)
    inner_act = (inner_value * sig).astype(jnp.bfloat16)
    grad_down = jnp.dot(inner_act.T, encoder_cotangent, preferred_element_type=jnp.float32) * factor
    d_act = jnp.dot(encoder_cotangent, w_down.T, preferred_element_type=jnp.float32)
    d_inner = (d_act * (sig + 1.702 * inner_value * sig * (1.0 - sig))).astype(jnp.bfloat16)
    grad_up = jnp.dot(normed.T, d_inner, preferred_element_type=jnp.float32) * factor
    return (grad_second, grad_first, grad_down, grad_up, encoder_cotangent)
```

```python
import math

import jax
import jax.numpy as jnp
from jax import lax
from jax.experimental import pallas as pl
from jax.experimental.pallas import tpu as pltpu
from jax.sharding import PartitionSpec as P

MESH = pl.DeviceIdType.MESH
BF = jnp.bfloat16
F32 = jnp.float32
NX, NY, NZ = 4, 4, 8
K = 8
FEAT, NORM, ENC = K, K + 1, K + 2


def dot_nn(left, right):
    return lax.dot_general(left, right, (((1,), (0,)), ((), ())), preferred_element_type=F32)


def dot_nt(left, right):
    return lax.dot_general(left, right, (((1,), (1,)), ((), ())), preferred_element_type=F32)


def dot_tn(left, right):
    return lax.dot_general(left, right, (((0,), (0,)), ((), ())), preferred_element_type=F32)


def device(x, y, z, core):
    return {"dp": y * 8 + (z // 2) * 2 + core, "tensor": lax.rem(z, 2) * 4 + x}


def wait(ref, sem):
    pltpu.make_async_copy(ref, ref, sem).wait()


def send(src, dst, send_sem, recv_sem, to):
    pltpu.make_async_remote_copy(
        src_ref=src, dst_ref=dst, send_sem=send_sem, recv_sem=recv_sem, device_id=to, device_id_type=MESH
    ).start()


def kernel(
    cot_in, feat_in, norm_in, preh_in, prei_in, w1_in, w2_in, wd_in,
    o_gs, o_small, o_enc,
    cot, w2, w1, wd, preh, prei, feat, norm, hact_t, slope, dhid, dpre,
    encp, encc, encs, encr, enc, iact, dinner,
    gsp, gsr, gsy, gsz, smp, smr, smy, smz,
    ag_s, ag_r, cot_l, w2_l, fn_l,
    w2_s, w2_r, w_s, w1_r, wd_r, pre_s, pre_r,
    ec_s, ec_r, ex_s, ex_r,
    gy_s, gy_r, gz_s, gz_r, sy_s, sy_r, sz_s, sz_r,
):
    dp, tensor = lax.axis_index("dp"), lax.axis_index("tensor")
    y, zh, c = dp // 8, lax.rem(dp // 2, 4), lax.rem(dp, 2)
    a, x = tensor // 4, lax.rem(tensor, 4)
    z = 2 * zh + a
    home = a == c
    xp, xm, x2 = lax.rem(x + 1, NX), lax.rem(x + 3, NX), lax.rem(x + 2, NX)
    right, left, other = device(xp, y, z, c), device(xm, y, z, c), device(x, y, z, 1 - c)
    partner_z = z + 1 - 2 * a
    outer_z = lax.rem(z + 2 * a - 1 + NZ, NZ)
    partner, outer = device(x, y, partner_z, a), device(x, y, outer_z, a)
    mine = c * 4 + x

    def rows_of(ref, shard, start=0, size=128):
        return ref.at[pl.ds(pl.multiple_of(shard * 128 + start, 64), size)]

    def view(item):
        if isinstance(item, int) and item >= K:
            return {FEAT: feat, NORM: norm, ENC: enc}[item]
        return cot.at[item]

    pltpu.make_async_copy(feat_in, rows_of(feat, mine), fn_l.at[0]).start()
    pltpu.make_async_copy(norm_in, rows_of(norm, mine), fn_l.at[1]).start()

    @pl.loop(0, K)
    def _(k):
        for quarter in range(4):
            cols = pl.ds(pl.multiple_of(quarter * 1024 + ((k % 4) * 2 + k // 4) * 128, 128), 128)
            to = pl.ds(quarter * 128, 128)
            pltpu.make_async_copy(
                cot_in.at[:, cols],
                cot.at[k, pl.ds(pl.multiple_of(mine * 128, 128), 128), to],
                cot_l.at[k],
            ).start()
            pltpu.make_async_copy(w2_in.at[:, cols], w2.at[a, k, :, to], w2_l.at[k]).start()

    barrier = pltpu.get_barrier_semaphore()
    friends = [right, left, device(x2, y, z, c), other]
    friends += [device(x, lax.rem(y + o, NY), z, c) for o in (1, 2, 3)]
    friends += [device(x, y, lax.rem(z + o, NZ), core) for o in range(1, NZ) for core in (0, 1)]
    for friend in friends:
        pl.semaphore_signal(barrier, inc=1, device_id=friend, device_id_type=MESH)
    pl.semaphore_wait(barrier, len(friends))

    def gather_start(item):
        buf = view(item)
        own = rows_of(buf, mine)
        send(own, own, ag_s.at[item, 0], ag_r.at[item, 0], right)
        send(own, own, ag_s.at[item, 1], ag_r.at[item, 1], left)
        send(own, own, ag_s.at[item, 2], ag_r.at[item, 4], other)

    def gather_middle(item):
        buf = view(item)
        from_left, from_right = rows_of(buf, c * 4 + xm), rows_of(buf, c * 4 + xp)
        wait(from_left, ag_r.at[item, 0])
        half = rows_of(buf, c * 4 + xm, 0, 64)
        send(half, half, ag_s.at[item, 3], ag_r.at[item, 2], right)
        send(from_left, from_left, ag_s.at[item, 4], ag_r.at[item, 5], other)
        wait(from_right, ag_r.at[item, 1])
        half = rows_of(buf, c * 4 + xp, 64, 64)
        send(half, half, ag_s.at[item, 5], ag_r.at[item, 3], left)
        send(from_right, from_right, ag_s.at[item, 6], ag_r.at[item, 6], other)

    def gather_last(item):
        buf = view(item)
        far = rows_of(buf, c * 4 + x2)
        wait(rows_of(buf, c * 4 + x2, 0, 64), ag_r.at[item, 2])
        wait(rows_of(buf, c * 4 + x2, 64, 64), ag_r.at[item, 3])
        send(far, far, ag_s.at[item, 7], ag_r.at[item, 7], other)

    def gather_end(item):
        buf = view(item)
        for index, at in ((4, x), (5, xm), (6, xp), (7, x2)):
            wait(rows_of(buf, (1 - c) * 4 + at), ag_r.at[item, index])

    def gather_sent(item):
        buf = view(item)
        whole, half = rows_of(buf, mine), rows_of(buf, mine, 0, 64)
        for index in range(8):
            wait(half if index in (3, 5) else whole, ag_s.at[item, index])

    def weights_start(k):
        wait(w2.at[a, k], w2_l.at[k])
        for index, (start, to) in enumerate(((c * 128, outer), (256 + c * 128, partner))):
            piece = w2.at[a, k, pl.ds(pl.multiple_of(start, 128), 128)]
            send(piece, piece, w2_s.at[k, index], w2_r.at[k, 2 * index + c], to)

    def weights_end(k):
        @pl.when(jnp.logical_not(home))
        def _():
            for index in range(4):
                wait(w2.at[c, k, pl.ds(index * 128, 128)], w2_r.at[k, index])

    def chunk_start(k):
        wait(cot.at[k, pl.ds(pl.multiple_of(mine * 128, 128), 128)], cot_l.at[k])
        gather_start(k)
        weights_start(k)

    def halves_start(src, dst, size, sems, first, to):
        part = pl.ds(pl.multiple_of(c * size, size), size)
        send(src.at[part], dst.at[part], w_s.at[first], sems.at[c], to)

        @pl.when(home)
        def _():
            for index in range(2):
                rows = pl.ds(index * size, size)
                pltpu.make_async_copy(src.at[rows], dst.at[rows], sems.at[index]).start()

    def halves_end(dst, size, sems):
        for index in range(2):
            wait(dst.at[pl.ds(index * size, size)], sems.at[index])

    def pre_start(index, src, dst):
        to_rows = pl.ds(pl.multiple_of(c * 512, 512), 512)

        def part(low):
            return src.at[pl.ds(pl.multiple_of(low * 512, 512), 512)]

        send(part(1 - a), dst.at[to_rows], pre_s.at[index, 0], pre_r.at[index, c], partner)

        @pl.when(home)
        def _():
            pltpu.make_async_copy(part(a), dst.at[to_rows], pre_r.at[index, c]).start()

        @pl.when(jnp.logical_not(home))
        def _():
            send(part(a), dst.at[to_rows], pre_s.at[index, 1], pre_r.at[index, c], other)

    def pre_end(index, dst):
        for core in range(2):
            wait(dst.at[pl.ds(core * 512, 512)], pre_r.at[index, core])

    def hidden_parts():
        pre_end(0, preh)

        @pl.loop(0, 8)
        def _(r):
            rows = pl.ds(pl.multiple_of(r * 128, 128), 128)
            value = preh[rows, :].astype(F32)
            cdf = 0.5 * (1.0 + lax.erf(value * (1.0 / math.sqrt(2.0))))
            pdf = jnp.exp(-0.5 * value * value) * (1.0 / math.sqrt(2.0 * math.pi))
            slope[rows, :] = cdf + value * pdf
            hact_t[:, rows] = jnp.transpose(value * cdf).astype(BF)

    def inner_parts():
        pre_end(1, prei)

        @pl.loop(0, 8)
        def _(r):
            rows = pl.ds(pl.multiple_of(r * 128, 128), 128)
            value = prei[rows, :].astype(F32)
            sig = 1.0 / (1.0 + jnp.exp(-1.702 * value))
            iact[rows, :] = (value * sig).astype(BF)
            dhid[rows, :] = sig + 1.702 * value * sig * (1.0 - sig)

    def chunk_work(k):
        @pl.loop(0, 2)
        def _(r):
            rows = pl.ds(pl.multiple_of(r * 512, 512), 512)
            dhid[rows, :] += dot_nt(cot[k, rows, :], w2[c, k])

        for half in range(2):
            term = dot_nn(hact_t[...], cot[k, :, half * 256:(half + 1) * 256])
            gsp[k, 2 * half] = term[:, :128].astype(BF)
            gsp[k, 2 * half + 1] = term[:, 128:].astype(BF)
        for o in (1, 2, 3):
            to = lax.rem(y + o, NY)
            send(gsp.at[k, to], gsr.at[k, o - 1], gy_s.at[k, o - 1], gy_r.at[k, o - 1], device(x, to, z, c))

    def chunk_sum(k):
        for o in range(3):
            wait(gsr.at[k, o], gy_r.at[k, o])
        total = gsp[k, y].astype(F32)
        for o in range(3):
            total = total + gsr[k, o].astype(F32)
        gsy[k] = total.astype(BF)
        to_z, core = 2 * lax.rem(k, 4) + c, k // 4
        own = jnp.logical_and(to_z == z, core == c)

        @pl.when(own)
        def _():
            pltpu.make_async_copy(gsy.at[k], gsz.at[z], gz_r.at[z]).start()

        @pl.when(jnp.logical_not(own))
        def _():
            send(gsy.at[k], gsz.at[z], gz_s.at[k], gz_r.at[z], device(x, y, to_z, core))

    def chunk_sum_sent(k):
        own = jnp.logical_and(2 * lax.rem(k, 4) + c == z, k // 4 == c)

        @pl.when(jnp.logical_not(own))
        def _():
            wait(gsy.at[k], gz_s.at[k])

    def small_start(i):
        for o in (1, 2, 3):
            to = lax.rem(y + o, NY)
            send(
                smp.at[i, pl.ds(pl.multiple_of(to * 256, 256), 256)], smr.at[i, o - 1],
                sy_s.at[i, o - 1], sy_r.at[i, o - 1], device(x, to, z, c),
            )

    def small_piece(i, hi, core):
        return smy.at[i, pl.ds(hi * 64 + core * 32, 32)]

    def small_sum(i):
        for o in range(3):
            wait(smr.at[i, o], sy_r.at[i, o])
        total = smp[i, pl.ds(pl.multiple_of(y * 256, 256), 256), :].astype(F32)
        for o in range(3):
            total = total + smr[i, o].astype(F32)
        smy[i] = total.astype(BF)
        for hi in range(4):
            for core in range(2):
                to_z = 2 * hi + c
                own = jnp.logical_and(to_z == z, core == c)

                @pl.when(own)
                def _():
                    pltpu.make_async_copy(small_piece(i, hi, core), smz.at[i, z], sz_r.at[i, z]).start()

                @pl.when(jnp.logical_not(own))
                def _():
                    send(
                        small_piece(i, hi, core), smz.at[i, z],
                        sz_s.at[i, hi, core], sz_r.at[i, z], device(x, y, to_z, core),
                    )

    def small_end(i):
        total = jnp.zeros((32, 512), F32)
        for source in range(NZ):
            wait(smz.at[i, source], sz_r.at[i, source])
            total = total + smz[i, source].astype(F32)
        o_small[i] = total

    def small_sent(i):
        for o in range(3):
            wait(smr.at[i, o], sy_s.at[i, o])
        for hi in range(4):
            for core in range(2):
                own = jnp.logical_and(2 * hi + c == z, core == c)

                @pl.when(jnp.logical_not(own))
                def _():
                    wait(small_piece(i, hi, core), sz_s.at[i, hi, core])

    def row_product(i, left, right):
        for part in range(2):
            cols = slice(part * 512, (part + 1) * 512)
            smp[i, cols, :] = dot_tn(left[:, cols], right[...]).astype(BF)

    pre_start(0, preh_in, preh)
    chunk_start(0)
    chunk_start(1)
    dhid[...] = jnp.zeros_like(dhid)

    @pl.loop(0, K + 2)
    def _(t):
        @pl.when(t + 2 < K)
        def _():
            chunk_start(t + 2)

        @pl.when(t == 5)
        def _():
            halves_start(w1_in, w1, 512, w1_r, 0, outer)
            pre_start(1, prei_in, prei)

        @pl.when(t == 6)
        def _():
            halves_start(wd_in, wd, 256, wd_r, 1, outer)
            wait(rows_of(feat, mine), fn_l.at[0])
            gather_start(FEAT)

        @pl.when(t < K)
        def _():
            gather_middle(t)

        @pl.when(jnp.logical_and(t >= 1, t <= K))
        def _():
            gather_last(t - 1)

        @pl.when(t == 2)
        def _():
            hidden_parts()

        @pl.when(t >= 4)
        def _():
            chunk_sum(t - 4)

        @pl.when(t >= 2)
        def _():
            gather_end(t - 2)
            weights_end(t - 2)
            chunk_work(t - 2)

    @pl.loop(0, 4)
    def _(r):
        rows = pl.ds(pl.multiple_of(r * 256, 256), 256)
        dpre[rows, :] = (dhid[rows, :] * slope[rows, :]).astype(BF)

    halves_end(w1, 512, w1_r)

    def partials(core):
        for pair in range(2):
            rows = pl.ds(pl.multiple_of(core * 512 + pair * 256, 256), 256)
            term = dot_nt(dpre[rows, :], w1[...]).astype(BF)
            encp[core, 2 * pair] = term[:128]
            encp[core, 2 * pair + 1] = term[128:]

    partials(1 - c)
    for at in range(4):
        send(encp.at[1 - c, at], encc.at[at], ec_s.at[at], ec_r.at[at], other)
    gather_middle(FEAT)
    partials(c)
    for at in range(4):
        wait(encc.at[at], ec_r.at[at])
    for o in (2, 1, 3):
        to = lax.rem(x + o, NX)
        encs[o - 1] = (encp[c, to].astype(F32) + encc[to].astype(F32)).astype(BF)
        send(encs.at[o - 1], encr.at[o - 1], ex_s.at[o - 1], ex_r.at[o - 1], device(to, y, z, c))
    wait(rows_of(norm, mine), fn_l.at[1])
    gather_start(NORM)
    gather_last(FEAT)
    chunk_sum(K - 2)
    chunk_sum(K - 1)
    gather_end(FEAT)
    row_product(0, feat, dpre)
    small_start(0)
    inner_parts()
    total = encp[c, x].astype(F32) + encc[x].astype(F32)
    for o in range(3):
        wait(encr.at[o], ex_r.at[o])
        total = total + encr[o].astype(F32)
    own_rows = total.astype(BF)
    enc[pl.ds(pl.multiple_of(mine * 128, 128), 128), :] = own_rows
    o_enc[...] = own_rows
    gather_start(ENC)
    gather_middle(NORM)
    gather_middle(ENC)
    gather_last(ENC)
    gather_last(NORM)
    small_sum(0)
    gather_end(ENC)
    row_product(1, enc, iact)
    small_start(1)
    halves_end(wd, 256, wd_r)

    @pl.loop(0, 4)
    def _(r):
        rows = pl.ds(pl.multiple_of(r * 256, 256), 256)
        dinner[rows, :] = (dot_nt(enc[rows, :], wd[...]) * dhid[rows, :]).astype(BF)

    gather_end(NORM)
    row_product(2, norm, dinner)
    small_start(2)

    total = jnp.zeros((512, 128), F32)
    for source in range(NZ):
        wait(gsz.at[source], gz_r.at[source])
        total = total + gsz[source].astype(F32)
    o_gs[...] = total
    small_end(0)
    small_sum(1)
    small_sum(2)
    small_end(1)
    small_end(2)

    @pl.loop(0, K)
    def _(k):
        gather_sent(k)
        for index in range(2):
            wait(w2.at[a, k, pl.ds(0, 128)], w2_s.at[k, index])
        for o in range(3):
            wait(gsr.at[k, o], gy_s.at[k, o])
        chunk_sum_sent(k)

    for item in (FEAT, NORM, ENC):
        gather_sent(item)
    wait(w1.at[pl.ds(0, 512)], w_s.at[0])
    wait(wd.at[pl.ds(0, 256)], w_s.at[1])
    for index in range(2):
        wait(preh.at[pl.ds(0, 512)], pre_s.at[index, 0])

        @pl.when(jnp.logical_not(home))
        def _():
            wait(preh.at[pl.ds(0, 512)], pre_s.at[index, 1])

    for at in range(4):
        wait(encc.at[at], ec_s.at[at])
    for o in range(3):
        wait(encr.at[o], ex_s.at[o])
    for i in range(3):
        small_sent(i)


def on_device(cotangent, features, normed, pre_hidden, pre_inner, w_first, w_second, w_down):
    tok_rows = cotangent.shape[0]
    factor = 1.0 / math.sqrt(tok_rows * lax.axis_size("tensor") * lax.axis_size("dp"))
    dma = pltpu.SemaphoreType.DMA
    vmem = pltpu.VMEM
    gs, small, own_rows = pl.pallas_call(
        kernel,
        out_shape=(
            jax.ShapeDtypeStruct((512, 128), F32),
            jax.ShapeDtypeStruct((3, 32, 512), F32),
            jax.ShapeDtypeStruct((128, 1024), BF),
        ),
        in_specs=[pl.BlockSpec(memory_space=pl.ANY)] * 8,
        out_specs=(pl.BlockSpec(memory_space=pltpu.VMEM),) * 3,
        scratch_shapes=[
            vmem((K, 1024, 512), BF),
            vmem((2, K, 512, 512), BF),
            vmem((1024, 512), BF),
            vmem((512, 1024), BF),
            vmem((1024, 512), BF),
            vmem((1024, 512), BF),
            vmem((1024, 1024), BF),
            vmem((1024, 1024), BF),
            vmem((512, 1024), BF),
            vmem((1024, 512), F32),
            vmem((1024, 512), F32),
            vmem((1024, 512), BF),
            vmem((2, 4, 128, 1024), BF),
            vmem((4, 128, 1024), BF),
            vmem((3, 128, 1024), BF),
            vmem((3, 128, 1024), BF),
            vmem((1024, 1024), BF),
            vmem((1024, 512), BF),
            vmem((1024, 512), BF),
            vmem((K, 4, 512, 128), BF),
            vmem((K, 3, 512, 128), BF),
            vmem((K, 512, 128), BF),
            vmem((NZ, 512, 128), BF),
            vmem((3, 1024, 512), BF),
            vmem((3, 3, 256, 512), BF),
            vmem((3, 256, 512), BF),
            vmem((3, NZ, 32, 512), BF),
            dma((K + 3, 8)), dma((K + 3, 8)), dma((K,)), dma((K,)), dma((2,)),
            dma((K, 2)), dma((K, 4)), dma((2,)), dma((2,)), dma((2,)), dma((2, 2)), dma((2, 2)),
            dma((4,)), dma((4,)), dma((3,)), dma((3,)),
            dma((K, 3)), dma((K, 3)), dma((K,)), dma((NZ,)),
            dma((3, 3)), dma((3, 3)), dma((3, 4, 2)), dma((3, NZ)),
        ],
        compiler_params=pltpu.CompilerParams(
            collective_id=0, has_side_effects=True, vmem_limit_bytes=63 * 2**20
        ),
        name="backward",
    )(cotangent, features, normed, pre_hidden, pre_inner, w_first, w_second, w_down)
    gs, small = gs * factor, small * factor
    return (gs, small[0], small[1].T, small[2], own_rows)


def solution(mesh):
    return jax.shard_map(
        on_device,
        mesh=mesh,
        in_specs=(
            P(("dp", "tensor"), None),
            P(("dp", "tensor"), None),
            P(("dp", "tensor"), None),
            P("dp", "tensor"),
            P("dp", "tensor"),
            P(None, "tensor"),
            P("tensor", None),
            P("tensor", None),
        ),
        out_specs=(
            P("tensor", "dp"),
            P("dp", "tensor"),
            P("tensor", "dp"),
            P("dp", "tensor"),
            P(("dp", "tensor"), None),
        ),
        check_vma=False,
    )
```

```python
import functools
import math

import jax
import jax.numpy as jnp
from jax import lax
from jax.experimental import pallas as pl
from jax.experimental.pallas import tpu as pltpu
from jax.sharding import PartitionSpec as P

MESH = pl.DeviceIdType.MESH
BF = jnp.bfloat16
F32 = jnp.float32
NX, NY, NZ = 4, 4, 8
K = 8
FEAT, NORM, ENC = K, K + 1, K + 2


def dot_nn(left, right):
    return lax.dot_general(left, right, (((1,), (0,)), ((), ())), preferred_element_type=F32)


def dot_nt(left, right):
    return lax.dot_general(left, right, (((1,), (1,)), ((), ())), preferred_element_type=F32)


def dot_tn(left, right):
    return lax.dot_general(left, right, (((0,), (0,)), ((), ())), preferred_element_type=F32)


def device(x, y, z, core):
    return {"dp": y * 8 + (z // 2) * 2 + core, "tensor": lax.rem(z, 2) * 4 + x}


def wait(ref, sem):
    pltpu.make_async_copy(ref, ref, sem).wait()


def send(src, dst, send_sem, recv_sem, to):
    pltpu.make_async_remote_copy(
        src_ref=src, dst_ref=dst, send_sem=send_sem, recv_sem=recv_sem, device_id=to, device_id_type=MESH
    ).start()


def kernel(
    cot_in, feat_in, norm_in, preh_in, prei_in, w1_in, w2_in, wd_in,
    o_gs, o_small, o_enc,
    cot, w2, w1, wd, preh, prei, feat, norm, hact_t, slope, dhid, dpre,
    encp, encc, encs, encr, enc, iact, dinner,
    gsp, gsr, gsy, gsz, smp, smr, smy, smz,
    ag_s, ag_r, cot_l, w2_l, fn_l,
    w2_s, w2_r, w_s, w1_r, wd_r, pre_s, pre_r,
    ec_s, ec_r, ex_s, ex_r,
    gy_s, gy_r, gz_s, gz_r, sy_s, sy_r, sz_s, sz_r,
):
    dp, tensor = lax.axis_index("dp"), lax.axis_index("tensor")
    y, zh, c = dp // 8, lax.rem(dp // 2, 4), lax.rem(dp, 2)
    a, x = tensor // 4, lax.rem(tensor, 4)
    z = 2 * zh + a
    home = a == c
    xp, xm, x2 = lax.rem(x + 1, NX), lax.rem(x + 3, NX), lax.rem(x + 2, NX)
    right, left, other = device(xp, y, z, c), device(xm, y, z, c), device(x, y, z, 1 - c)
    partner_z = z + 1 - 2 * a
    outer_z = lax.rem(z + 2 * a - 1 + NZ, NZ)
    partner, outer = device(x, y, partner_z, a), device(x, y, outer_z, a)
    mine = c * 4 + x

    def rows_of(ref, shard, start=0, size=128):
        return ref.at[pl.ds(pl.multiple_of(shard * 128 + start, 64), size)]

    def view(item):
        if isinstance(item, int) and item >= K:
            return {FEAT: feat, NORM: norm, ENC: enc}[item]
        return cot.at[item]

    pltpu.make_async_copy(feat_in, rows_of(feat, mine), fn_l.at[0]).start()
    pltpu.make_async_copy(norm_in, rows_of(norm, mine), fn_l.at[1]).start()

    @pl.loop(0, K)
    def _(k):
        for quarter in range(4):
            cols = pl.ds(pl.multiple_of(quarter * 1024 + ((k % 4) * 2 + k // 4) * 128, 128), 128)
            to = pl.ds(quarter * 128, 128)
            pltpu.make_async_copy(
                cot_in.at[:, cols],
                cot.at[k, pl.ds(pl.multiple_of(mine * 128, 128), 128), to],
                cot_l.at[k],
            ).start()
            pltpu.make_async_copy(w2_in.at[:, cols], w2.at[a, k, :, to], w2_l.at[k]).start()

    barrier = pltpu.get_barrier_semaphore()
    friends = [right, left, device(x2, y, z, c), other]
    friends += [device(x, lax.rem(y + o, NY), z, c) for o in (1, 2, 3)]
    friends += [device(x, y, lax.rem(z + o, NZ), core) for o in range(1, NZ) for core in (0, 1)]
    for friend in friends:
        pl.semaphore_signal(barrier, inc=1, device_id=friend, device_id_type=MESH)
    pl.semaphore_wait(barrier, len(friends))

    def gather_start(item):
        buf = view(item)
        own = rows_of(buf, mine)
        send(own, own, ag_s.at[item, 0], ag_r.at[item, 0], right)
        send(own, own, ag_s.at[item, 1], ag_r.at[item, 1], left)
        send(own, own, ag_s.at[item, 2], ag_r.at[item, 4], other)

    def gather_middle(item):
        buf = view(item)
        from_left, from_right = rows_of(buf, c * 4 + xm), rows_of(buf, c * 4 + xp)
        wait(from_left, ag_r.at[item, 0])
        half = rows_of(buf, c * 4 + xm, 0, 64)
        send(half, half, ag_s.at[item, 3], ag_r.at[item, 2], right)
        send(from_left, from_left, ag_s.at[item, 4], ag_r.at[item, 5], other)
        wait(from_right, ag_r.at[item, 1])
        half = rows_of(buf, c * 4 + xp, 64, 64)
        send(half, half, ag_s.at[item, 5], ag_r.at[item, 3], left)
        send(from_right, from_right, ag_s.at[item, 6], ag_r.at[item, 6], other)

    def gather_last(item):
        buf = view(item)
        far = rows_of(buf, c * 4 + x2)
        wait(rows_of(buf, c * 4 + x2, 0, 64), ag_r.at[item, 2])
        wait(rows_of(buf, c * 4 + x2, 64, 64), ag_r.at[item, 3])
        send(far, far, ag_s.at[item, 7], ag_r.at[item, 7], other)

    def gather_end(item):
        buf = view(item)
        for index, at in ((4, x), (5, xm), (6, xp), (7, x2)):
            wait(rows_of(buf, (1 - c) * 4 + at), ag_r.at[item, index])

    def gather_sent(item):
        buf = view(item)
        whole, half = rows_of(buf, mine), rows_of(buf, mine, 0, 64)
        for index in range(8):
            wait(half if index in (3, 5) else whole, ag_s.at[item, index])

    def weights_start(k):
        wait(w2.at[a, k], w2_l.at[k])
        for index, (start, to) in enumerate(((c * 128, outer), (256 + c * 128, partner))):
            piece = w2.at[a, k, pl.ds(pl.multiple_of(start, 128), 128)]
            send(piece, piece, w2_s.at[k, index], w2_r.at[k, 2 * index + c], to)

    def weights_end(k):
        @pl.when(jnp.logical_not(home))
        def _():
            for index in range(4):
                wait(w2.at[c, k, pl.ds(index * 128, 128)], w2_r.at[k, index])

    def chunk_start(k):
        wait(cot.at[k, pl.ds(pl.multiple_of(mine * 128, 128), 128)], cot_l.at[k])
        gather_start(k)

    def halves_start(src, dst, size, sems, first, to):
        part = pl.ds(pl.multiple_of(c * size, size), size)
        send(src.at[part], dst.at[part], w_s.at[first], sems.at[c], to)

        @pl.when(home)
        def _():
            for index in range(2):
                rows = pl.ds(index * size, size)
                pltpu.make_async_copy(src.at[rows], dst.at[rows], sems.at[index]).start()

    def halves_end(dst, size, sems):
        for index in range(2):
            wait(dst.at[pl.ds(index * size, size)], sems.at[index])

    def pre_start(index, src, dst):
        to_rows = pl.ds(pl.multiple_of(c * 512, 512), 512)

        def part(low):
            return src.at[pl.ds(pl.multiple_of(low * 512, 512), 512)]

        send(part(1 - a), dst.at[to_rows], pre_s.at[index, 0], pre_r.at[index, c], partner)

        @pl.when(home)
        def _():
            pltpu.make_async_copy(part(a), dst.at[to_rows], pre_r.at[index, c]).start()

        @pl.when(jnp.logical_not(home))
        def _():
            send(part(a), dst.at[to_rows], pre_s.at[index, 1], pre_r.at[index, c], other)

    def pre_end(index, dst):
        for core in range(2):
            wait(dst.at[pl.ds(core * 512, 512)], pre_r.at[index, core])

    def hidden_parts():
        pre_end(0, preh)

        @pl.loop(0, 8)
        def _(r):
            rows = pl.ds(pl.multiple_of(r * 128, 128), 128)
            value = preh[rows, :].astype(F32)
            cdf = 0.5 * (1.0 + lax.erf(value * (1.0 / math.sqrt(2.0))))
            pdf = jnp.exp(-0.5 * value * value) * (1.0 / math.sqrt(2.0 * math.pi))
            slope[rows, :] = cdf + value * pdf
            hact_t[:, rows] = jnp.transpose(value * cdf).astype(BF)

    def inner_parts():
        pre_end(1, prei)

        @pl.loop(0, 8)
        def _(r):
            rows = pl.ds(pl.multiple_of(r * 128, 128), 128)
            value = prei[rows, :].astype(F32)
            sig = 1.0 / (1.0 + jnp.exp(-1.702 * value))
            iact[rows, :] = (value * sig).astype(BF)
            dhid[rows, :] = sig + 1.702 * value * sig * (1.0 - sig)

    def chunk_work(k):
        @pl.loop(0, 2)
        def _(r):
            rows = pl.ds(pl.multiple_of(r * 512, 512), 512)
            dhid[rows, :] += dot_nt(cot[k, rows, :], w2[c, k])

        for half in range(2):
            term = dot_nn(hact_t[...], cot[k, :, half * 256:(half + 1) * 256])
            gsp[k, 2 * half] = term[:, :128].astype(BF)
            gsp[k, 2 * half + 1] = term[:, 128:].astype(BF)
        for o in (1, 2, 3):
            to = lax.rem(y + o, NY)
            send(gsp.at[k, to], gsr.at[k, o - 1], gy_s.at[k, o - 1], gy_r.at[k, o - 1], device(x, to, z, c))

    def chunk_sum(k):
        for o in range(3):
            wait(gsr.at[k, o], gy_r.at[k, o])
        total = gsp[k, y].astype(F32)
        for o in range(3):
            total = total + gsr[k, o].astype(F32)
        gsy[k] = total.astype(BF)
        to_z, core = 2 * lax.rem(k, 4) + c, k // 4
        own = jnp.logical_and(to_z == z, core == c)

        @pl.when(own)
        def _():
            pltpu.make_async_copy(gsy.at[k], gsz.at[z], gz_r.at[z]).start()

        @pl.when(jnp.logical_not(own))
        def _():
            send(gsy.at[k], gsz.at[z], gz_s.at[k], gz_r.at[z], device(x, y, to_z, core))

    def chunk_sum_sent(k):
        own = jnp.logical_and(2 * lax.rem(k, 4) + c == z, k // 4 == c)

        @pl.when(jnp.logical_not(own))
        def _():
            wait(gsy.at[k], gz_s.at[k])

    def small_start(i):
        for o in (1, 2, 3):
            to = lax.rem(y + o, NY)
            send(
                smp.at[i, pl.ds(pl.multiple_of(to * 256, 256), 256)], smr.at[i, o - 1],
                sy_s.at[i, o - 1], sy_r.at[i, o - 1], device(x, to, z, c),
            )

    def small_piece(i, hi, core):
        return smy.at[i, pl.ds(hi * 64 + core * 32, 32)]

    def small_sum(i):
        for o in range(3):
            wait(smr.at[i, o], sy_r.at[i, o])
        total = smp[i, pl.ds(pl.multiple_of(y * 256, 256), 256), :].astype(F32)
        for o in range(3):
            total = total + smr[i, o].astype(F32)
        smy[i] = total.astype(BF)
        for hi in range(4):
            for core in range(2):
                to_z = 2 * hi + c
                own = jnp.logical_and(to_z == z, core == c)

                @pl.when(own)
                def _():
                    pltpu.make_async_copy(small_piece(i, hi, core), smz.at[i, z], sz_r.at[i, z]).start()

                @pl.when(jnp.logical_not(own))
                def _():
                    send(
                        small_piece(i, hi, core), smz.at[i, z],
                        sz_s.at[i, hi, core], sz_r.at[i, z], device(x, y, to_z, core),
                    )

    def small_end(i):
        total = jnp.zeros((32, 512), F32)
        for source in range(NZ):
            wait(smz.at[i, source], sz_r.at[i, source])
            total = total + smz[i, source].astype(F32)
        o_small[i] = total

    def small_sent(i):
        for o in range(3):
            wait(smr.at[i, o], sy_s.at[i, o])
        for hi in range(4):
            for core in range(2):
                own = jnp.logical_and(2 * hi + c == z, core == c)

                @pl.when(jnp.logical_not(own))
                def _():
                    wait(small_piece(i, hi, core), sz_s.at[i, hi, core])

    def row_product(i, left, right):
        for part in range(2):
            cols = slice(part * 512, (part + 1) * 512)
            smp[i, cols, :] = dot_tn(left[:, cols], right[...]).astype(BF)

    chunk_start(0)
    weights_start(0)
    pre_start(0, preh_in, preh)
    chunk_start(1)
    weights_start(1)
    weights_start(2)
    dhid[...] = jnp.zeros_like(dhid)

    @pl.loop(0, K + 2)
    def _(t):
        @pl.when(t + 2 < K)
        def _():
            chunk_start(t + 2)

        @pl.when(t + 3 < K)
        def _():
            weights_start(t + 3)

        @pl.when(t == 3)
        def _():
            halves_start(w1_in, w1, 512, w1_r, 0, outer)

        @pl.when(t == 6)
        def _():
            pre_start(1, prei_in, prei)

        @pl.when(t == 7)
        def _():
            halves_start(wd_in, wd, 256, wd_r, 1, outer)

        @pl.when(t == 8)
        def _():
            wait(rows_of(feat, mine), fn_l.at[0])
            gather_start(FEAT)

        @pl.when(t < K)
        def _():
            gather_middle(t)

        @pl.when(jnp.logical_and(t >= 1, t <= K))
        def _():
            gather_last(t - 1)

        @pl.when(t == 2)
        def _():
            hidden_parts()

        @pl.when(t >= 2)
        def _():
            gather_end(t - 2)
            weights_end(t - 2)
            chunk_work(t - 2)

    @pl.loop(0, 4)
    def _(r):
        rows = pl.ds(pl.multiple_of(r * 256, 256), 256)
        dpre[rows, :] = (dhid[rows, :] * slope[rows, :]).astype(BF)

    halves_end(w1, 512, w1_r)

    def partials(core):
        for pair in range(2):
            rows = pl.ds(pl.multiple_of(core * 512 + pair * 256, 256), 256)
            term = dot_nt(dpre[rows, :], w1[...]).astype(BF)
            encp[core, 2 * pair] = term[:128]
            encp[core, 2 * pair + 1] = term[128:]

    partials(1 - c)
    for at in range(4):
        send(encp.at[1 - c, at], encc.at[at], ec_s.at[at], ec_r.at[at], other)
    gather_middle(FEAT)
    partials(c)
    for at in range(4):
        wait(encc.at[at], ec_r.at[at])
    for o in (2, 1, 3):
        to = lax.rem(x + o, NX)
        encs[o - 1] = (encp[c, to].astype(F32) + encc[to].astype(F32)).astype(BF)
        send(encs.at[o - 1], encr.at[o - 1], ex_s.at[o - 1], ex_r.at[o - 1], device(to, y, z, c))
    wait(rows_of(norm, mine), fn_l.at[1])
    gather_start(NORM)
    chunk_sum(0)
    chunk_sum(1)
    chunk_sum(2)
    gather_last(FEAT)
    chunk_sum(3)
    chunk_sum(4)
    gather_end(FEAT)
    row_product(0, feat, dpre)
    small_start(0)
    chunk_sum(5)
    inner_parts()
    total = encp[c, x].astype(F32) + encc[x].astype(F32)
    for o in range(3):
        wait(encr.at[o], ex_r.at[o])
        total = total + encr[o].astype(F32)
    own_rows = total.astype(BF)
    enc[pl.ds(pl.multiple_of(mine * 128, 128), 128), :] = own_rows
    o_enc[...] = own_rows
    gather_start(ENC)
    chunk_sum(6)
    chunk_sum(7)
    gather_middle(NORM)
    gather_middle(ENC)
    gather_last(ENC)
    gather_last(NORM)
    small_sum(0)
    gather_end(ENC)
    row_product(1, enc, iact)
    small_start(1)
    halves_end(wd, 256, wd_r)

    @pl.loop(0, 4)
    def _(r):
        rows = pl.ds(pl.multiple_of(r * 256, 256), 256)
        dinner[rows, :] = (dot_nt(enc[rows, :], wd[...]) * dhid[rows, :]).astype(BF)

    gather_end(NORM)
    row_product(2, norm, dinner)
    small_start(2)

    total = jnp.zeros((512, 128), F32)
    for source in range(NZ):
        wait(gsz.at[source], gz_r.at[source])
        total = total + gsz[source].astype(F32)
    o_gs[...] = total
    small_end(0)
    small_sum(1)
    small_sum(2)
    small_end(1)
    small_end(2)

    @pl.loop(0, K)
    def _(k):
        gather_sent(k)
        for index in range(2):
            wait(w2.at[a, k, pl.ds(0, 128)], w2_s.at[k, index])
        for o in range(3):
            wait(gsr.at[k, o], gy_s.at[k, o])
        chunk_sum_sent(k)

    for item in (FEAT, NORM, ENC):
        gather_sent(item)
    wait(w1.at[pl.ds(0, 512)], w_s.at[0])
    wait(wd.at[pl.ds(0, 256)], w_s.at[1])
    for index in range(2):
        wait(preh.at[pl.ds(0, 512)], pre_s.at[index, 0])

        @pl.when(jnp.logical_not(home))
        def _():
            wait(preh.at[pl.ds(0, 512)], pre_s.at[index, 1])

    for at in range(4):
        wait(encc.at[at], ec_s.at[at])
    for o in range(3):
        wait(encr.at[o], ex_s.at[o])
    for i in range(3):
        small_sent(i)


def finish(gs, small, own_rows, o_gs, o_first, o_down, o_up, o_enc, *, factor):
    o_gs[...] = gs[...] * factor
    o_first[...] = small[0] * factor
    o_down[...] = jnp.transpose(small[1] * factor)
    o_up[...] = small[2] * factor
    o_enc[...] = own_rows[...]


def on_device(cotangent, features, normed, pre_hidden, pre_inner, w_first, w_second, w_down):
    tok_rows = cotangent.shape[0]
    factor = 1.0 / math.sqrt(tok_rows * lax.axis_size("tensor") * lax.axis_size("dp"))
    dma = pltpu.SemaphoreType.DMA
    vmem = pltpu.VMEM
    gs, small, own_rows = pl.pallas_call(
        kernel,
        out_shape=(
            jax.ShapeDtypeStruct((512, 128), F32),
            jax.ShapeDtypeStruct((3, 32, 512), F32),
            jax.ShapeDtypeStruct((128, 1024), BF),
        ),
        in_specs=[pl.BlockSpec(memory_space=pl.ANY)] * 8,
        out_specs=(pl.BlockSpec(memory_space=pltpu.VMEM),) * 3,
        scratch_shapes=[
            vmem((K, 1024, 512), BF),
            vmem((2, K, 512, 512), BF),
            vmem((1024, 512), BF),
            vmem((512, 1024), BF),
            vmem((1024, 512), BF),
            vmem((1024, 512), BF),
            vmem((1024, 1024), BF),
            vmem((1024, 1024), BF),
            vmem((512, 1024), BF),
            vmem((1024, 512), F32),
            vmem((1024, 512), F32),
            vmem((1024, 512), BF),
            vmem((2, 4, 128, 1024), BF),
            vmem((4, 128, 1024), BF),
            vmem((3, 128, 1024), BF),
            vmem((3, 128, 1024), BF),
            vmem((1024, 1024), BF),
            vmem((1024, 512), BF),
            vmem((1024, 512), BF),
            vmem((K, 4, 512, 128), BF),
            vmem((K, 3, 512, 128), BF),
            vmem((K, 512, 128), BF),
            vmem((NZ, 512, 128), BF),
            vmem((3, 1024, 512), BF),
            vmem((3, 3, 256, 512), BF),
            vmem((3, 256, 512), BF),
            vmem((3, NZ, 32, 512), BF),
            dma((K + 3, 8)), dma((K + 3, 8)), dma((K,)), dma((K,)), dma((2,)),
            dma((K, 2)), dma((K, 4)), dma((2,)), dma((2,)), dma((2,)), dma((2, 2)), dma((2, 2)),
            dma((4,)), dma((4,)), dma((3,)), dma((3,)),
            dma((K, 3)), dma((K, 3)), dma((K,)), dma((NZ,)),
            dma((3, 3)), dma((3, 3)), dma((3, 4, 2)), dma((3, NZ)),
        ],
        compiler_params=pltpu.CompilerParams(
            collective_id=0, has_side_effects=True, vmem_limit_bytes=63 * 2**20
        ),
        name="backward",
    )(cotangent, features, normed, pre_hidden, pre_inner, w_first, w_second, w_down)
    return pl.pallas_call(
        functools.partial(finish, factor=factor),
        out_shape=(
            jax.ShapeDtypeStruct((512, 128), F32),
            jax.ShapeDtypeStruct((32, 512), F32),
            jax.ShapeDtypeStruct((512, 32), F32),
            jax.ShapeDtypeStruct((32, 512), F32),
            jax.ShapeDtypeStruct((128, 1024), BF),
        ),
        name="finish",
    )(gs, small, own_rows)


def solution(mesh):
    return jax.shard_map(
        on_device,
        mesh=mesh,
        in_specs=(
            P(("dp", "tensor"), None),
            P(("dp", "tensor"), None),
            P(("dp", "tensor"), None),
            P("dp", "tensor"),
            P("dp", "tensor"),
            P(None, "tensor"),
            P("tensor", None),
            P("tensor", None),
        ),
        out_specs=(
            P("tensor", "dp"),
            P("dp", "tensor"),
            P("tensor", "dp"),
            P("dp", "tensor"),
            P(("dp", "tensor"), None),
        ),
        check_vma=False,
    )
```

```python
import functools
import math

import jax
import jax.numpy as jnp
from jax import lax
from jax.experimental import pallas as pl
from jax.experimental.pallas import tpu as pltpu
from jax.sharding import PartitionSpec as P

MESH = pl.DeviceIdType.MESH
BF = jnp.bfloat16
F32 = jnp.float32
NX, NY, NZ = 4, 4, 8
K = 8
FEAT, NORM, ENC = K, K + 1, K + 2


def dot_nn(left, right):
    return lax.dot_general(left, right, (((1,), (0,)), ((), ())), preferred_element_type=F32)


def dot_nt(left, right):
    return lax.dot_general(left, right, (((1,), (1,)), ((), ())), preferred_element_type=F32)


def dot_tn(left, right):
    return lax.dot_general(left, right, (((0,), (0,)), ((), ())), preferred_element_type=F32)


def device(x, y, z, core):
    return {"dp": y * 8 + (z // 2) * 2 + core, "tensor": lax.rem(z, 2) * 4 + x}


def wait(ref, sem):
    pltpu.make_async_copy(ref, ref, sem).wait()


def send(src, dst, send_sem, recv_sem, to):
    pltpu.make_async_remote_copy(
        src_ref=src, dst_ref=dst, send_sem=send_sem, recv_sem=recv_sem, device_id=to, device_id_type=MESH
    ).start()


def kernel(
    cot_in, feat_in, norm_in, preh_in, prei_in, w1_in, w2_in, wd_in,
    o_gs, o_small, o_enc,
    cot, w2, w1, wd, preh, prei, feat, norm, hact_t, slope, dhid, dpre,
    encp, encc, encs, encr, enc, iact, dinner,
    gsp, gsr, gsy, gsz, smp, smr, smy, smz, sdp, sdr, sdy, sdz,
    ag_s, ag_r, cot_l, w2_l, fn_l,
    w2_s, w2_r, w_s, w1_r, wd_r, pre_s, pre_r,
    ec_s, ec_r, ex_s, ex_r,
    gy_s, gy_r, gz_s, gz_r, sy_s, sy_r, sz_s, sz_r, dz_s, dz_r, dy_s, dy_r,
):
    dp, tensor = lax.axis_index("dp"), lax.axis_index("tensor")
    y, zh, c = dp // 8, lax.rem(dp // 2, 4), lax.rem(dp, 2)
    a, x = tensor // 4, lax.rem(tensor, 4)
    z = 2 * zh + a
    home = a == c
    xp, xm, x2 = lax.rem(x + 1, NX), lax.rem(x + 3, NX), lax.rem(x + 2, NX)
    right, left, other = device(xp, y, z, c), device(xm, y, z, c), device(x, y, z, 1 - c)
    partner_z = z + 1 - 2 * a
    outer_z = lax.rem(z + 2 * a - 1 + NZ, NZ)
    partner, outer = device(x, y, partner_z, a), device(x, y, outer_z, a)
    mine = c * 4 + x

    def rows_of(ref, shard, start=0, size=128):
        return ref.at[pl.ds(pl.multiple_of(shard * 128 + start, 64), size)]

    def view(item):
        if isinstance(item, int) and item >= K:
            return {FEAT: feat, NORM: norm, ENC: enc}[item]
        return cot.at[item]

    pltpu.make_async_copy(feat_in, rows_of(feat, mine), fn_l.at[0]).start()
    pltpu.make_async_copy(norm_in, rows_of(norm, mine), fn_l.at[1]).start()

    @pl.loop(0, K)
    def _(k):
        for quarter in range(4):
            cols = pl.ds(pl.multiple_of(quarter * 1024 + ((k % 4) * 2 + k // 4) * 128, 128), 128)
            to = pl.ds(quarter * 128, 128)
            pltpu.make_async_copy(
                cot_in.at[:, cols],
                cot.at[k, pl.ds(pl.multiple_of(mine * 128, 128), 128), to],
                cot_l.at[k],
            ).start()
            pltpu.make_async_copy(w2_in.at[:, cols], w2.at[a, k, :, to], w2_l.at[k]).start()

    barrier = pltpu.get_barrier_semaphore()
    friends = [right, left, device(x2, y, z, c), other]
    friends += [device(x, lax.rem(y + o, NY), z, core) for o in (1, 2, 3) for core in (c, 1 - c)]
    friends += [device(x, y, lax.rem(z + o, NZ), core) for o in range(1, NZ) for core in (0, 1)]
    for friend in friends:
        pl.semaphore_signal(barrier, inc=1, device_id=friend, device_id_type=MESH)
    pl.semaphore_wait(barrier, len(friends))

    def gather_start(item):
        buf = view(item)
        own = rows_of(buf, mine)
        send(own, own, ag_s.at[item, 0], ag_r.at[item, 0], right)
        send(own, own, ag_s.at[item, 1], ag_r.at[item, 1], left)
        send(own, own, ag_s.at[item, 2], ag_r.at[item, 4], other)

    def gather_middle(item):
        buf = view(item)
        from_left, from_right = rows_of(buf, c * 4 + xm), rows_of(buf, c * 4 + xp)
        wait(from_left, ag_r.at[item, 0])
        half = rows_of(buf, c * 4 + xm, 0, 64)
        send(half, half, ag_s.at[item, 3], ag_r.at[item, 2], right)
        send(from_left, from_left, ag_s.at[item, 4], ag_r.at[item, 5], other)
        wait(from_right, ag_r.at[item, 1])
        half = rows_of(buf, c * 4 + xp, 64, 64)
        send(half, half, ag_s.at[item, 5], ag_r.at[item, 3], left)
        send(from_right, from_right, ag_s.at[item, 6], ag_r.at[item, 6], other)

    def gather_last(item):
        buf = view(item)
        far = rows_of(buf, c * 4 + x2)
        wait(rows_of(buf, c * 4 + x2, 0, 64), ag_r.at[item, 2])
        wait(rows_of(buf, c * 4 + x2, 64, 64), ag_r.at[item, 3])
        send(far, far, ag_s.at[item, 7], ag_r.at[item, 7], other)

    def gather_end(item):
        buf = view(item)
        for index, at in ((4, x), (5, xm), (6, xp), (7, x2)):
            wait(rows_of(buf, (1 - c) * 4 + at), ag_r.at[item, index])

    def gather_sent(item):
        buf = view(item)
        whole, half = rows_of(buf, mine), rows_of(buf, mine, 0, 64)
        for index in range(8):
            wait(half if index in (3, 5) else whole, ag_s.at[item, index])

    def weights_start(k):
        wait(w2.at[a, k], w2_l.at[k])
        for index, (start, to) in enumerate(((c * 128, outer), (256 + c * 128, partner))):
            piece = w2.at[a, k, pl.ds(pl.multiple_of(start, 128), 128)]
            send(piece, piece, w2_s.at[k, index], w2_r.at[k, 2 * index + c], to)

    def weights_end(k):
        @pl.when(jnp.logical_not(home))
        def _():
            for index in range(4):
                wait(w2.at[c, k, pl.ds(index * 128, 128)], w2_r.at[k, index])

    def chunk_start(k):
        wait(cot.at[k, pl.ds(pl.multiple_of(mine * 128, 128), 128)], cot_l.at[k])
        gather_start(k)

    def halves_start(src, dst, size, sems, first, to):
        part = pl.ds(pl.multiple_of(c * size, size), size)
        send(src.at[part], dst.at[part], w_s.at[first], sems.at[c], to)

        @pl.when(home)
        def _():
            for index in range(2):
                rows = pl.ds(index * size, size)
                pltpu.make_async_copy(src.at[rows], dst.at[rows], sems.at[index]).start()

    def halves_end(dst, size, sems):
        for index in range(2):
            wait(dst.at[pl.ds(index * size, size)], sems.at[index])

    def pre_start(index, src, dst):
        to_rows = pl.ds(pl.multiple_of(c * 512, 512), 512)

        def part(low):
            return src.at[pl.ds(pl.multiple_of(low * 512, 512), 512)]

        send(part(1 - a), dst.at[to_rows], pre_s.at[index, 0], pre_r.at[index, c], partner)

        @pl.when(home)
        def _():
            pltpu.make_async_copy(part(a), dst.at[to_rows], pre_r.at[index, c]).start()

        @pl.when(jnp.logical_not(home))
        def _():
            send(part(a), dst.at[to_rows], pre_s.at[index, 1], pre_r.at[index, c], other)

    def pre_end(index, dst):
        for core in range(2):
            wait(dst.at[pl.ds(core * 512, 512)], pre_r.at[index, core])

    def hidden_parts():
        pre_end(0, preh)

        @pl.loop(0, 8)
        def _(r):
            rows = pl.ds(pl.multiple_of(r * 128, 128), 128)
            value = preh[rows, :].astype(F32)
            cdf = 0.5 * (1.0 + lax.erf(value * (1.0 / math.sqrt(2.0))))
            pdf = jnp.exp(-0.5 * value * value) * (1.0 / math.sqrt(2.0 * math.pi))
            slope[rows, :] = cdf + value * pdf
            hact_t[:, rows] = jnp.transpose(value * cdf).astype(BF)

    def inner_parts():
        pre_end(1, prei)

        @pl.loop(0, 8)
        def _(r):
            rows = pl.ds(pl.multiple_of(r * 128, 128), 128)
            value = prei[rows, :].astype(F32)
            sig = 1.0 / (1.0 + jnp.exp(-1.702 * value))
            iact[rows, :] = (value * sig).astype(BF)
            dhid[rows, :] = sig + 1.702 * value * sig * (1.0 - sig)

    def chunk_work(k):
        @pl.loop(0, 2)
        def _(r):
            rows = pl.ds(pl.multiple_of(r * 512, 512), 512)
            dhid[rows, :] += dot_nt(cot[k, rows, :], w2[c, k])

    def chunk_grad(k):
        for half in range(2):
            term = dot_nn(hact_t[...], cot[k, :, half * 256:(half + 1) * 256])
            gsp[k, 2 * half] = term[:, :128].astype(BF)
            gsp[k, 2 * half + 1] = term[:, 128:].astype(BF)
        for o in (1, 2, 3):
            to = lax.rem(y + o, NY)
            send(gsp.at[k, to], gsr.at[k, o - 1], gy_s.at[k, o - 1], gy_r.at[k, o - 1], device(x, to, z, c))

    def chunk_sum(k):
        for o in range(3):
            wait(gsr.at[k, o], gy_r.at[k, o])
        total = gsp[k, y].astype(F32)
        for o in range(3):
            total = total + gsr[k, o].astype(F32)
        gsy[k] = total.astype(BF)
        to_z, core = 2 * lax.rem(k, 4) + c, k // 4
        own = jnp.logical_and(to_z == z, core == c)

        @pl.when(own)
        def _():
            pltpu.make_async_copy(gsy.at[k], gsz.at[z], gz_r.at[z]).start()

        @pl.when(jnp.logical_not(own))
        def _():
            send(gsy.at[k], gsz.at[z], gz_s.at[k], gz_r.at[z], device(x, y, to_z, core))

    def chunk_sum_sent(k):
        own = jnp.logical_and(2 * lax.rem(k, 4) + c == z, k // 4 == c)

        @pl.when(jnp.logical_not(own))
        def _():
            wait(gsy.at[k], gz_s.at[k])

    def width(i):
        return pl.ds(0, 512 if i == 0 else 384)

    def small_send(i, to):
        o = lax.rem(to - y + NY, NY)
        send(
            smp.at[i, pl.ds(pl.multiple_of(to * 256, 256), 256), width(i)], smr.at[i, o - 1, :, width(i)],
            sy_s.at[i, o - 1], sy_r.at[i, o - 1], device(x, to, z, c),
        )

    def small_piece(i, hi, core):
        return smy.at[i, pl.ds(hi * 64 + core * 32, 32), width(i)]

    def small_sum(i):
        total = smp[i, pl.ds(pl.multiple_of(y * 256, 256), 256), width(i)].astype(F32)
        for o in range(3):
            wait(smr.at[i, o, :, width(i)], sy_r.at[i, o])
            total = total + smr[i, o, :, width(i)].astype(F32)
        smy[i, :, width(i)] = total.astype(BF)
        for hi in range(4):
            for core in range(2):
                to_z = 2 * hi + c
                own = jnp.logical_and(to_z == z, core == c)
                to = smz.at[i, z, :, width(i)]

                @pl.when(own)
                def _():
                    pltpu.make_async_copy(small_piece(i, hi, core), to, sz_r.at[i, z]).start()

                @pl.when(jnp.logical_not(own))
                def _():
                    send(
                        small_piece(i, hi, core), to,
                        sz_s.at[i, hi, core], sz_r.at[i, z], device(x, y, to_z, core),
                    )

    def small_end(i):
        total = None
        for source in range(NZ):
            wait(smz.at[i, source, :, width(i)], sz_r.at[i, source])
            term = smz[i, source, :, width(i)].astype(F32)
            total = term if total is None else total + term
        o_small[i, :, width(i)] = total

    def small_sent(i):
        for o in range(3):
            wait(smr.at[i, o, :, width(i)], sy_s.at[i, o])
        for hi in range(4):
            for core in range(2):
                own = jnp.logical_and(2 * hi + c == z, core == c)

                @pl.when(jnp.logical_not(own))
                def _():
                    wait(small_piece(i, hi, core), sz_s.at[i, hi, core])

    def side_start(j):
        for hi in range(4):
            to_z = 2 * hi + c

            @pl.when(to_z != z)
            def _():
                send(sdp.at[j, hi], sdr.at[j, z], dz_s.at[j, hi], dz_r.at[j, z], device(x, y, to_z, c))

    def side_sum(j):
        @pl.when(home)
        def _():
            sdr[j, z] = sdp[j, zh]
            total = jnp.zeros((256, 128), F32)
            for source in range(NZ):
                @pl.when(source != z)
                def _():
                    wait(sdr.at[j, source], dz_r.at[j, source])

            for source in range(NZ):
                total = total + sdr[j, source].astype(F32)
            sdy[j] = total.astype(BF)
            for o in range(NY):
                to = lax.rem(y + o, NY)
                for flip in range(2):
                    core = c if flip == 0 else 1 - c
                    piece = sdy.at[j, pl.ds(pl.multiple_of(to * 64 + core * 32, 32), 32)]
                    if o == 0 and flip == 0:
                        pltpu.make_async_copy(piece, sdz.at[j, y], dy_r.at[j, y]).start()
                    else:
                        send(piece, sdz.at[j, y], dy_s.at[j, o, flip], dy_r.at[j, y], device(x, to, z, core))

    def side_end(j):
        total = None
        for source in range(NY):
            wait(sdz.at[j, source], dy_r.at[j, source])
            term = sdz[j, source].astype(F32)
            total = term if total is None else total + term
        o_small[j + 1, :, 384:] = total

    def side_sent(j):
        for hi in range(4):
            @pl.when(2 * hi + c != z)
            def _():
                wait(sdp.at[j, hi], dz_s.at[j, hi])

        @pl.when(home)
        def _():
            for o in range(NY):
                for flip in range(2):
                    if o + flip > 0:
                        wait(sdz.at[j, 0], dy_s.at[j, o, flip])

    def row_store(i, part, term):
        smp[i, part * 512:(part + 1) * 512, :] = term.astype(BF)
        if i > 0:
            for two in range(2):
                for hi in range(4):
                    at = (2 * part + two) * 64
                    sdp[i - 1, hi, at:at + 64, :] = term[two * 256 + hi * 64:two * 256 + hi * 64 + 64, 384:].astype(BF)

    def row_product(i, left, right):
        for part in range(2):
            cols = slice(part * 512, (part + 1) * 512)
            row_store(i, part, dot_tn(left[:, cols], right[...]))
            for to in (2 * part, 2 * part + 1):
                @pl.when(y != to)
                def _():
                    small_send(i, to)

    chunk_start(0)
    weights_start(0)
    pre_start(0, preh_in, preh)
    chunk_start(1)
    weights_start(1)
    weights_start(2)
    dhid[...] = jnp.zeros_like(dhid)

    @pl.loop(0, K + 2)
    def _(t):
        @pl.when(t + 3 < K)
        def _():
            weights_start(t + 3)

        @pl.when(t == 3)
        def _():
            halves_start(w1_in, w1, 512, w1_r, 0, outer)

        @pl.when(t == 6)
        def _():
            pre_start(1, prei_in, prei)

        @pl.when(t == 7)
        def _():
            halves_start(wd_in, wd, 256, wd_r, 1, outer)

        @pl.when(t == 8)
        def _():
            wait(rows_of(feat, mine), fn_l.at[0])
            gather_start(FEAT)

        @pl.when(t < K)
        def _():
            gather_middle(t)

        @pl.when(t + 2 < K)
        def _():
            chunk_start(t + 2)

        @pl.when(jnp.logical_and(t >= 1, t <= K))
        def _():
            gather_last(t - 1)

        @pl.when(t == 2)
        def _():
            hidden_parts()

        @pl.when(t >= 2)
        def _():
            gather_end(t - 2)
            weights_end(t - 2)
            chunk_work(t - 2)

        @pl.when(jnp.logical_and(t >= 2, t <= K))
        def _():
            chunk_grad(t - 2)

    def slopes(core):
        for part in range(2):
            rows = pl.ds(pl.multiple_of(core * 512 + part * 256, 256), 256)
            dpre[rows, :] = (dhid[rows, :] * slope[rows, :]).astype(BF)

    slopes(1 - c)
    halves_end(w1, 512, w1_r)

    def partials(core):
        for pair in range(2):
            rows = pl.ds(pl.multiple_of(core * 512 + pair * 256, 256), 256)
            term = dot_nt(dpre[rows, :], w1[...]).astype(BF)
            encp[core, 2 * pair] = term[:128]
            encp[core, 2 * pair + 1] = term[128:]

    partials(1 - c)
    for at in range(4):
        send(encp.at[1 - c, at], encc.at[at], ec_s.at[at], ec_r.at[at], other)
    slopes(c)
    partials(c)
    gather_middle(FEAT)
    for at in range(4):
        wait(encc.at[at], ec_r.at[at])
    for o in (2, 1, 3):
        to = lax.rem(x + o, NX)
        encs[o - 1] = (encp[c, to].astype(F32) + encc[to].astype(F32)).astype(BF)
        send(encs.at[o - 1], encr.at[o - 1], ex_s.at[o - 1], ex_r.at[o - 1], device(to, y, z, c))
    wait(rows_of(norm, mine), fn_l.at[1])
    gather_start(NORM)
    chunk_grad(K - 1)
    chunk_sum(0)
    chunk_sum(1)
    chunk_sum(2)
    gather_last(FEAT)
    chunk_sum(3)
    chunk_sum(4)
    gather_end(FEAT)
    row_product(0, feat, dpre)
    chunk_sum(5)
    inner_parts()
    total = encp[c, x].astype(F32) + encc[x].astype(F32)
    for o in range(3):
        wait(encr.at[o], ex_r.at[o])
        total = total + encr[o].astype(F32)
    own_rows = total.astype(BF)
    enc[pl.ds(pl.multiple_of(mine * 128, 128), 128), :] = own_rows
    o_enc[...] = own_rows
    gather_start(ENC)
    chunk_sum(6)
    chunk_sum(7)
    gather_middle(NORM)
    gather_middle(ENC)
    gather_last(ENC)
    gather_last(NORM)
    small_sum(0)
    gather_end(ENC)
    row_product(1, enc, iact)
    side_start(0)
    halves_end(wd, 256, wd_r)

    @pl.loop(0, 4)
    def _(r):
        rows = pl.ds(pl.multiple_of(r * 256, 256), 256)
        dinner[rows, :] = (dot_nt(enc[rows, :], wd[...]) * dhid[rows, :]).astype(BF)

    gather_end(NORM)
    row_product(2, norm, dinner)
    side_start(1)

    total = jnp.zeros((512, 128), F32)
    for source in range(NZ):
        wait(gsz.at[source], gz_r.at[source])
        total = total + gsz[source].astype(F32)
    o_gs[...] = total
    small_end(0)
    side_sum(0)
    small_sum(1)
    side_sum(1)
    small_sum(2)
    small_end(1)
    side_end(0)
    side_end(1)
    small_end(2)

    @pl.loop(0, K)
    def _(k):
        gather_sent(k)
        for index in range(2):
            wait(w2.at[a, k, pl.ds(0, 128)], w2_s.at[k, index])
        for o in range(3):
            wait(gsr.at[k, o], gy_s.at[k, o])
        chunk_sum_sent(k)

    for item in (FEAT, NORM, ENC):
        gather_sent(item)
    wait(w1.at[pl.ds(0, 512)], w_s.at[0])
    wait(wd.at[pl.ds(0, 256)], w_s.at[1])
    for index in range(2):
        wait(preh.at[pl.ds(0, 512)], pre_s.at[index, 0])

        @pl.when(jnp.logical_not(home))
        def _():
            wait(preh.at[pl.ds(0, 512)], pre_s.at[index, 1])

    for at in range(4):
        wait(encc.at[at], ec_s.at[at])
    for o in range(3):
        wait(encr.at[o], ex_s.at[o])
    for i in range(3):
        small_sent(i)
    for j in range(2):
        side_sent(j)


def finish(gs, small, own_rows, o_gs, o_first, o_down, o_up, o_enc, *, factor):
    o_gs[...] = gs[...] * factor
    o_first[...] = small[0] * factor
    o_down[...] = small[1] * factor
    o_up[...] = small[2] * factor
    o_enc[...] = own_rows[...]


def on_device(cotangent, features, normed, pre_hidden, pre_inner, w_first, w_second, w_down):
    tok_rows = cotangent.shape[0]
    factor = 1.0 / math.sqrt(tok_rows * lax.axis_size("tensor") * lax.axis_size("dp"))
    dma = pltpu.SemaphoreType.DMA
    vmem = pltpu.VMEM
    gs, small, own_rows = pl.pallas_call(
        kernel,
        out_shape=(
            jax.ShapeDtypeStruct((512, 128), F32),
            jax.ShapeDtypeStruct((3, 32, 512), F32),
            jax.ShapeDtypeStruct((128, 1024), BF),
        ),
        in_specs=[pl.BlockSpec(memory_space=pl.ANY)] * 8,
        out_specs=(pl.BlockSpec(memory_space=pltpu.VMEM),) * 3,
        scratch_shapes=[
            vmem((K, 1024, 512), BF),
            vmem((2, K, 512, 512), BF),
            vmem((1024, 512), BF),
            vmem((512, 1024), BF),
            vmem((1024, 512), BF),
            vmem((1024, 512), BF),
            vmem((1024, 1024), BF),
            vmem((1024, 1024), BF),
            vmem((512, 1024), BF),
            vmem((1024, 512), F32),
            vmem((1024, 512), F32),
            vmem((1024, 512), BF),
            vmem((2, 4, 128, 1024), BF),
            vmem((4, 128, 1024), BF),
            vmem((3, 128, 1024), BF),
            vmem((3, 128, 1024), BF),
            vmem((1024, 1024), BF),
            vmem((1024, 512), BF),
            vmem((1024, 512), BF),
            vmem((K, 4, 512, 128), BF),
            vmem((K, 3, 512, 128), BF),
            vmem((K, 512, 128), BF),
            vmem((NZ, 512, 128), BF),
            vmem((3, 1024, 512), BF),
            vmem((3, 3, 256, 512), BF),
            vmem((3, 256, 512), BF),
            vmem((3, NZ, 32, 512), BF),
            vmem((2, 4, 256, 128), BF),
            vmem((2, NZ, 256, 128), BF),
            vmem((2, 256, 128), BF),
            vmem((2, NY, 32, 128), BF),
            dma((K + 3, 8)), dma((K + 3, 8)), dma((K,)), dma((K,)), dma((2,)),
            dma((K, 2)), dma((K, 4)), dma((2,)), dma((2,)), dma((2,)), dma((2, 2)), dma((2, 2)),
            dma((4,)), dma((4,)), dma((3,)), dma((3,)),
            dma((K, 3)), dma((K, 3)), dma((K,)), dma((NZ,)),
            dma((3, 3)), dma((3, 3)), dma((3, 4, 2)), dma((3, NZ)),
            dma((2, 4)), dma((2, NZ)), dma((2, NY, 2)), dma((2, NY)),
        ],
        compiler_params=pltpu.CompilerParams(
            collective_id=0, has_side_effects=True, vmem_limit_bytes=63 * 2**20
        ),
        name="backward",
    )(cotangent, features, normed, pre_hidden, pre_inner, w_first, w_second, w_down)
    grad_second, first, down_rows, grad_up, enc_rows = pl.pallas_call(
        functools.partial(finish, factor=factor),
        out_shape=(
            jax.ShapeDtypeStruct((512, 128), F32),
            jax.ShapeDtypeStruct((32, 512), F32),
            jax.ShapeDtypeStruct((32, 512), F32),
            jax.ShapeDtypeStruct((32, 512), F32),
            jax.ShapeDtypeStruct((128, 1024), BF),
        ),
        name="finish",
    )(gs, small, own_rows)
    return (grad_second, first, down_rows.T, grad_up, enc_rows)


def solution(mesh):
    return jax.shard_map(
        on_device,
        mesh=mesh,
        in_specs=(
            P(("dp", "tensor"), None),
            P(("dp", "tensor"), None),
            P(("dp", "tensor"), None),
            P("dp", "tensor"),
            P("dp", "tensor"),
            P(None, "tensor"),
            P("tensor", None),
            P("tensor", None),
        ),
        out_specs=(
            P("tensor", "dp"),
            P("dp", "tensor"),
            P("tensor", "dp"),
            P("dp", "tensor"),
            P(("dp", "tensor"), None),
        ),
        check_vma=False,
    )
```

```python
import functools
import math

import jax
import jax.numpy as jnp
from jax import lax
from jax.experimental import pallas as pl
from jax.experimental.pallas import tpu as pltpu
from jax.sharding import PartitionSpec as P

MESH = pl.DeviceIdType.MESH
BF = jnp.bfloat16
F32 = jnp.float32
NX, NY, NZ = 4, 4, 8
K = 8
FEAT, NORM, ENC = K, K + 1, K + 2


def dot_nn(left, right):
    return lax.dot_general(left, right, (((1,), (0,)), ((), ())), preferred_element_type=F32)


def dot_nt(left, right):
    return lax.dot_general(left, right, (((1,), (1,)), ((), ())), preferred_element_type=F32)


def dot_tn(left, right):
    return lax.dot_general(left, right, (((0,), (0,)), ((), ())), preferred_element_type=F32)


def device(x, y, z, core):
    return {"dp": y * 8 + (z // 2) * 2 + core, "tensor": lax.rem(z, 2) * 4 + x}


def wait(ref, sem):
    pltpu.make_async_copy(ref, ref, sem).wait()


def send(src, dst, send_sem, recv_sem, to):
    pltpu.make_async_remote_copy(
        src_ref=src, dst_ref=dst, send_sem=send_sem, recv_sem=recv_sem, device_id=to, device_id_type=MESH
    ).start()


def kernel(
    cot_in, feat_in, norm_in, preh_in, prei_in, w1_in, w2_in, wd_in,
    o_gs, o_small, o_enc,
    cot, w2, w1, wd, preh, prei, feat, norm, hact_t, slope, dhid, dpre,
    encp, encc, encs, encr, enc, iact, dinner,
    gsp, gsr, gsy, gsz, smp, smr, smy, smz, sdp, sdr, sdy, sdz,
    ag_s, ag_r, cot_l, w2_l, fn_l,
    w2_s, w2_r, w_s, w1_r, wd_r, pre_s, pre_r,
    ec_s, ec_r, ex_s, ex_r,
    gy_s, gy_r, gz_s, gz_r, sy_s, sy_r, sz_s, sz_r, dz_s, dz_r, dy_s, dy_r,
):
    dp, tensor = lax.axis_index("dp"), lax.axis_index("tensor")
    y, zh, c = dp // 8, lax.rem(dp // 2, 4), lax.rem(dp, 2)
    a, x = tensor // 4, lax.rem(tensor, 4)
    z = 2 * zh + a
    home = a == c
    xp, xm, x2 = lax.rem(x + 1, NX), lax.rem(x + 3, NX), lax.rem(x + 2, NX)
    right, left, other = device(xp, y, z, c), device(xm, y, z, c), device(x, y, z, 1 - c)
    partner_z = z + 1 - 2 * a
    outer_z = lax.rem(z + 2 * a - 1 + NZ, NZ)
    partner, outer = device(x, y, partner_z, a), device(x, y, outer_z, a)
    mine = c * 4 + x

    def rows_of(ref, shard, start=0, size=128):
        return ref.at[pl.ds(pl.multiple_of(shard * 128 + start, 64), size)]

    def view(item):
        if isinstance(item, int) and item >= K:
            return {FEAT: feat, NORM: norm, ENC: enc}[item]
        return cot.at[item]

    pltpu.make_async_copy(feat_in, rows_of(feat, mine), fn_l.at[0]).start()
    pltpu.make_async_copy(norm_in, rows_of(norm, mine), fn_l.at[1]).start()

    @pl.loop(0, K)
    def _(k):
        for quarter in range(4):
            cols = pl.ds(pl.multiple_of(quarter * 1024 + ((k % 4) * 2 + k // 4) * 128, 128), 128)
            to = pl.ds(quarter * 128, 128)
            pltpu.make_async_copy(
                cot_in.at[:, cols],
                cot.at[k, pl.ds(pl.multiple_of(mine * 128, 128), 128), to],
                cot_l.at[k],
            ).start()
            pltpu.make_async_copy(w2_in.at[:, cols], w2.at[a, k, :, to], w2_l.at[k]).start()

    barrier = pltpu.get_barrier_semaphore()
    friends = [right, left, device(x2, y, z, c), other]
    friends += [device(x, lax.rem(y + o, NY), z, core) for o in (1, 2, 3) for core in (c, 1 - c)]
    friends += [device(x, y, lax.rem(z + o, NZ), core) for o in range(1, NZ) for core in (0, 1)]
    for friend in friends:
        pl.semaphore_signal(barrier, inc=1, device_id=friend, device_id_type=MESH)
    pl.semaphore_wait(barrier, len(friends))

    def gather_start(item):
        buf = view(item)
        own = rows_of(buf, mine)
        send(own, own, ag_s.at[item, 0], ag_r.at[item, 0], right)
        send(own, own, ag_s.at[item, 1], ag_r.at[item, 1], left)

    def gather_middle(item):
        buf = view(item)
        from_left, from_right = rows_of(buf, c * 4 + xm), rows_of(buf, c * 4 + xp)
        wait(from_left, ag_r.at[item, 0])
        half = rows_of(buf, c * 4 + xm, 0, 64)
        send(half, half, ag_s.at[item, 3], ag_r.at[item, 2], right)
        send(from_left, from_left, ag_s.at[item, 4], ag_r.at[item, 5], other)
        wait(from_right, ag_r.at[item, 1])
        half = rows_of(buf, c * 4 + xp, 64, 64)
        send(half, half, ag_s.at[item, 5], ag_r.at[item, 3], left)
        send(from_right, from_right, ag_s.at[item, 6], ag_r.at[item, 6], other)
        own = rows_of(buf, mine)
        send(own, own, ag_s.at[item, 2], ag_r.at[item, 4], other)

    def gather_last(item):
        buf = view(item)
        far = rows_of(buf, c * 4 + x2)
        wait(rows_of(buf, c * 4 + x2, 0, 64), ag_r.at[item, 2])
        wait(rows_of(buf, c * 4 + x2, 64, 64), ag_r.at[item, 3])
        send(far, far, ag_s.at[item, 7], ag_r.at[item, 7], other)

    def gather_end(item):
        buf = view(item)
        for index, at in ((4, x), (5, xm), (6, xp), (7, x2)):
            wait(rows_of(buf, (1 - c) * 4 + at), ag_r.at[item, index])

    def gather_sent(item):
        buf = view(item)
        whole, half = rows_of(buf, mine), rows_of(buf, mine, 0, 64)
        for index in range(8):
            wait(half if index in (3, 5) else whole, ag_s.at[item, index])

    def weights_start(k):
        wait(w2.at[a, k], w2_l.at[k])
        for index, (start, to) in enumerate(((c * 128, outer), (256 + c * 128, partner))):
            piece = w2.at[a, k, pl.ds(pl.multiple_of(start, 128), 128)]
            send(piece, piece, w2_s.at[k, index], w2_r.at[k, 2 * index + c], to)

    def weights_end(k):
        @pl.when(jnp.logical_not(home))
        def _():
            for index in range(4):
                wait(w2.at[c, k, pl.ds(index * 128, 128)], w2_r.at[k, index])

    def chunk_start(k):
        wait(cot.at[k, pl.ds(pl.multiple_of(mine * 128, 128), 128)], cot_l.at[k])
        gather_start(k)

    def halves_start(src, dst, size, sems, first, to):
        part = pl.ds(pl.multiple_of(c * size, size), size)
        send(src.at[part], dst.at[part], w_s.at[first], sems.at[c], to)

        @pl.when(home)
        def _():
            for index in range(2):
                rows = pl.ds(index * size, size)
                pltpu.make_async_copy(src.at[rows], dst.at[rows], sems.at[index]).start()

    def halves_end(dst, size, sems):
        for index in range(2):
            wait(dst.at[pl.ds(index * size, size)], sems.at[index])

    def pre_start(index, src, dst):
        to_rows = pl.ds(pl.multiple_of(c * 512, 512), 512)

        def part(low):
            return src.at[pl.ds(pl.multiple_of(low * 512, 512), 512)]

        send(part(1 - a), dst.at[to_rows], pre_s.at[index, 0], pre_r.at[index, c], partner)

        @pl.when(home)
        def _():
            pltpu.make_async_copy(part(a), dst.at[to_rows], pre_r.at[index, c]).start()

        @pl.when(jnp.logical_not(home))
        def _():
            send(part(a), dst.at[to_rows], pre_s.at[index, 1], pre_r.at[index, c], other)

    def pre_end(index, dst):
        for core in range(2):
            wait(dst.at[pl.ds(core * 512, 512)], pre_r.at[index, core])

    def hidden_parts():
        pre_end(0, preh)

        @pl.loop(0, 8)
        def _(r):
            rows = pl.ds(pl.multiple_of(r * 128, 128), 128)
            value = preh[rows, :].astype(F32)
            cdf = 0.5 * (1.0 + lax.erf(value * (1.0 / math.sqrt(2.0))))
            pdf = jnp.exp(-0.5 * value * value) * (1.0 / math.sqrt(2.0 * math.pi))
            slope[rows, :] = cdf + value * pdf
            hact_t[:, rows] = jnp.transpose(value * cdf).astype(BF)

    def inner_parts():
        pre_end(1, prei)

        @pl.loop(0, 8)
        def _(r):
            rows = pl.ds(pl.multiple_of(r * 128, 128), 128)
            value = prei[rows, :].astype(F32)
            sig = 1.0 / (1.0 + jnp.exp(-1.702 * value))
            iact[rows, :] = (value * sig).astype(BF)
            dhid[rows, :] = sig + 1.702 * value * sig * (1.0 - sig)

    def chunk_work(k):
        @pl.loop(0, 2)
        def _(r):
            rows = pl.ds(pl.multiple_of(r * 512, 512), 512)
            dhid[rows, :] += dot_nt(cot[k, rows, :], w2[c, k])

    def chunk_grad(k):
        for half in range(2):
            term = dot_nn(hact_t[...], cot[k, :, half * 256:(half + 1) * 256])
            gsp[k, 2 * half] = term[:, :128].astype(BF)
            gsp[k, 2 * half + 1] = term[:, 128:].astype(BF)
        for o in (1, 2, 3):
            to = lax.rem(y + o, NY)
            send(gsp.at[k, to], gsr.at[k, o - 1], gy_s.at[k, o - 1], gy_r.at[k, o - 1], device(x, to, z, c))

    def chunk_sum(k):
        for o in range(3):
            wait(gsr.at[k, o], gy_r.at[k, o])
        total = gsp[k, y].astype(F32)
        for o in range(3):
            total = total + gsr[k, o].astype(F32)
        gsy[k] = total.astype(BF)
        to_z, core = 2 * lax.rem(k, 4) + c, k // 4
        own = jnp.logical_and(to_z == z, core == c)

        @pl.when(own)
        def _():
            pltpu.make_async_copy(gsy.at[k], gsz.at[z], gz_r.at[z]).start()

        @pl.when(jnp.logical_not(own))
        def _():
            send(gsy.at[k], gsz.at[z], gz_s.at[k], gz_r.at[z], device(x, y, to_z, core))

    def chunk_sum_sent(k):
        own = jnp.logical_and(2 * lax.rem(k, 4) + c == z, k // 4 == c)

        @pl.when(jnp.logical_not(own))
        def _():
            wait(gsy.at[k], gz_s.at[k])

    def width(i):
        return pl.ds(0, 512 if i == 0 else 384)

    def small_send(i, to):
        o = lax.rem(to - y + NY, NY)
        send(
            smp.at[i, pl.ds(pl.multiple_of(to * 256, 256), 256), width(i)], smr.at[i, o - 1, :, width(i)],
            sy_s.at[i, o - 1], sy_r.at[i, o - 1], device(x, to, z, c),
        )

    def small_piece(i, hi, core):
        return smy.at[i, pl.ds(hi * 64 + core * 32, 32), width(i)]

    def small_sum(i):
        total = smp[i, pl.ds(pl.multiple_of(y * 256, 256), 256), width(i)].astype(F32)
        for o in range(3):
            wait(smr.at[i, o, :, width(i)], sy_r.at[i, o])
            total = total + smr[i, o, :, width(i)].astype(F32)
        smy[i, :, width(i)] = total.astype(BF)
        for hi in range(4):
            for core in range(2):
                to_z = 2 * hi + c
                own = jnp.logical_and(to_z == z, core == c)
                to = smz.at[i, z, :, width(i)]

                @pl.when(own)
                def _():
                    pltpu.make_async_copy(small_piece(i, hi, core), to, sz_r.at[i, z]).start()

                @pl.when(jnp.logical_not(own))
                def _():
                    send(
                        small_piece(i, hi, core), to,
                        sz_s.at[i, hi, core], sz_r.at[i, z], device(x, y, to_z, core),
                    )

    def small_end(i):
        total = None
        for source in range(NZ):
            wait(smz.at[i, source, :, width(i)], sz_r.at[i, source])
            term = smz[i, source, :, width(i)].astype(F32)
            total = term if total is None else total + term
        o_small[i, :, width(i)] = total

    def small_sent(i):
        for o in range(3):
            wait(smr.at[i, o, :, width(i)], sy_s.at[i, o])
        for hi in range(4):
            for core in range(2):
                own = jnp.logical_and(2 * hi + c == z, core == c)

                @pl.when(jnp.logical_not(own))
                def _():
                    wait(small_piece(i, hi, core), sz_s.at[i, hi, core])

    def side_start(j):
        for hi in range(4):
            to_z = 2 * hi + c

            @pl.when(to_z != z)
            def _():
                send(sdp.at[j, hi], sdr.at[j, z], dz_s.at[j, hi], dz_r.at[j, z], device(x, y, to_z, c))

    def side_sum(j):
        @pl.when(home)
        def _():
            sdr[j, z] = sdp[j, zh]
            total = jnp.zeros((256, 128), F32)
            for source in range(NZ):
                @pl.when(source != z)
                def _():
                    wait(sdr.at[j, source], dz_r.at[j, source])

            for source in range(NZ):
                total = total + sdr[j, source].astype(F32)
            sdy[j] = total.astype(BF)
            for o in range(NY):
                to = lax.rem(y + o, NY)
                for flip in range(2):
                    core = c if flip == 0 else 1 - c
                    piece = sdy.at[j, pl.ds(pl.multiple_of(to * 64 + core * 32, 32), 32)]
                    if o == 0 and flip == 0:
                        pltpu.make_async_copy(piece, sdz.at[j, y], dy_r.at[j, y]).start()
                    else:
                        send(piece, sdz.at[j, y], dy_s.at[j, o, flip], dy_r.at[j, y], device(x, to, z, core))

    def side_end(j):
        total = None
        for source in range(NY):
            wait(sdz.at[j, source], dy_r.at[j, source])
            term = sdz[j, source].astype(F32)
            total = term if total is None else total + term
        o_small[j + 1, :, 384:] = total

    def side_sent(j):
        for hi in range(4):
            @pl.when(2 * hi + c != z)
            def _():
                wait(sdp.at[j, hi], dz_s.at[j, hi])

        @pl.when(home)
        def _():
            for o in range(NY):
                for flip in range(2):
                    if o + flip > 0:
                        wait(sdz.at[j, 0], dy_s.at[j, o, flip])

    def row_store(i, part, term):
        smp[i, part * 512:(part + 1) * 512, :] = term.astype(BF)
        if i > 0:
            for two in range(2):
                for hi in range(4):
                    at = (2 * part + two) * 64
                    sdp[i - 1, hi, at:at + 64, :] = term[two * 256 + hi * 64:two * 256 + hi * 64 + 64, 384:].astype(BF)

    def row_product(i, left, right):
        for part in range(2):
            cols = slice(part * 512, (part + 1) * 512)
            row_store(i, part, dot_tn(left[:, cols], right[...]))
            for to in (2 * part, 2 * part + 1):
                @pl.when(y != to)
                def _():
                    small_send(i, to)

    chunk_start(0)
    weights_start(0)
    pre_start(0, preh_in, preh)
    chunk_start(1)
    weights_start(1)
    weights_start(2)
    dhid[...] = jnp.zeros_like(dhid)

    @pl.loop(0, K + 2)
    def _(t):
        @pl.when(t + 3 < K)
        def _():
            weights_start(t + 3)

        @pl.when(t == 3)
        def _():
            halves_start(w1_in, w1, 512, w1_r, 0, outer)

        @pl.when(t == 6)
        def _():
            pre_start(1, prei_in, prei)

        @pl.when(t == 7)
        def _():
            halves_start(wd_in, wd, 256, wd_r, 1, outer)

        @pl.when(t == 8)
        def _():
            wait(rows_of(feat, mine), fn_l.at[0])
            gather_start(FEAT)

        @pl.when(t < K)
        def _():
            gather_middle(t)

        @pl.when(t + 2 < K)
        def _():
            chunk_start(t + 2)

        @pl.when(jnp.logical_and(t >= 1, t <= K))
        def _():
            gather_last(t - 1)

        @pl.when(t == 2)
        def _():
            hidden_parts()

        @pl.when(t >= 2)
        def _():
            gather_end(t - 2)
            weights_end(t - 2)
            chunk_work(t - 2)

        @pl.when(jnp.logical_and(t >= 2, t <= K))
        def _():
            chunk_grad(t - 2)

    def slopes(core):
        for part in range(2):
            rows = pl.ds(pl.multiple_of(core * 512 + part * 256, 256), 256)
            dpre[rows, :] = (dhid[rows, :] * slope[rows, :]).astype(BF)

    slopes(1 - c)
    halves_end(w1, 512, w1_r)

    def partials(core):
        for pair in range(2):
            rows = pl.ds(pl.multiple_of(core * 512 + pair * 256, 256), 256)
            term = dot_nt(dpre[rows, :], w1[...]).astype(BF)
            encp[core, 2 * pair] = term[:128]
            encp[core, 2 * pair + 1] = term[128:]

    partials(1 - c)
    for at in range(4):
        send(encp.at[1 - c, at], encc.at[at], ec_s.at[at], ec_r.at[at], other)
    slopes(c)
    partials(c)
    gather_middle(FEAT)
    for at in range(4):
        wait(encc.at[at], ec_r.at[at])
    for o in (2, 1, 3):
        to = lax.rem(x + o, NX)
        encs[o - 1] = (encp[c, to].astype(F32) + encc[to].astype(F32)).astype(BF)
        send(encs.at[o - 1], encr.at[o - 1], ex_s.at[o - 1], ex_r.at[o - 1], device(to, y, z, c))
    wait(rows_of(norm, mine), fn_l.at[1])
    gather_start(NORM)
    chunk_grad(K - 1)
    chunk_sum(0)
    chunk_sum(1)
    chunk_sum(2)
    gather_last(FEAT)
    chunk_sum(3)
    chunk_sum(4)
    gather_end(FEAT)
    row_product(0, feat, dpre)
    chunk_sum(5)
    inner_parts()
    total = encp[c, x].astype(F32) + encc[x].astype(F32)
    for o in range(3):
        wait(encr.at[o], ex_r.at[o])
        total = total + encr[o].astype(F32)
    own_rows = total.astype(BF)
    enc[pl.ds(pl.multiple_of(mine * 128, 128), 128), :] = own_rows
    o_enc[...] = own_rows
    gather_start(ENC)
    chunk_sum(6)
    chunk_sum(7)
    gather_middle(NORM)
    gather_middle(ENC)
    gather_last(ENC)
    gather_last(NORM)
    small_sum(0)
    gather_end(ENC)
    row_product(1, enc, iact)
    side_start(0)
    halves_end(wd, 256, wd_r)

    @pl.loop(0, 4)
    def _(r):
        rows = pl.ds(pl.multiple_of(r * 256, 256), 256)
        dinner[rows, :] = (dot_nt(enc[rows, :], wd[...]) * dhid[rows, :]).astype(BF)

    gather_end(NORM)
    row_product(2, norm, dinner)
    side_start(1)

    total = jnp.zeros((512, 128), F32)
    for source in range(NZ):
        wait(gsz.at[source], gz_r.at[source])
        total = total + gsz[source].astype(F32)
    o_gs[...] = total
    small_end(0)
    side_sum(0)
    small_sum(1)
    side_sum(1)
    small_sum(2)
    small_end(1)
    side_end(0)
    side_end(1)
    small_end(2)

    @pl.loop(0, K)
    def _(k):
        gather_sent(k)
        for index in range(2):
            wait(w2.at[a, k, pl.ds(0, 128)], w2_s.at[k, index])
        for o in range(3):
            wait(gsr.at[k, o], gy_s.at[k, o])
        chunk_sum_sent(k)

    for item in (FEAT, NORM, ENC):
        gather_sent(item)
    wait(w1.at[pl.ds(0, 512)], w_s.at[0])
    wait(wd.at[pl.ds(0, 256)], w_s.at[1])
    for index in range(2):
        wait(preh.at[pl.ds(0, 512)], pre_s.at[index, 0])

        @pl.when(jnp.logical_not(home))
        def _():
            wait(preh.at[pl.ds(0, 512)], pre_s.at[index, 1])

    for at in range(4):
        wait(encc.at[at], ec_s.at[at])
    for o in range(3):
        wait(encr.at[o], ex_s.at[o])
    for i in range(3):
        small_sent(i)
    for j in range(2):
        side_sent(j)


def finish(gs, small, own_rows, o_gs, o_first, o_down, o_up, o_enc, *, factor):
    o_gs[...] = gs[...] * factor
    o_first[...] = small[0] * factor
    o_down[...] = small[1] * factor
    o_up[...] = small[2] * factor
    o_enc[...] = own_rows[...]


def on_device(cotangent, features, normed, pre_hidden, pre_inner, w_first, w_second, w_down):
    tok_rows = cotangent.shape[0]
    factor = 1.0 / math.sqrt(tok_rows * lax.axis_size("tensor") * lax.axis_size("dp"))
    dma = pltpu.SemaphoreType.DMA
    vmem = pltpu.VMEM
    gs, small, own_rows = pl.pallas_call(
        kernel,
        out_shape=(
            jax.ShapeDtypeStruct((512, 128), F32),
            jax.ShapeDtypeStruct((3, 32, 512), F32),
            jax.ShapeDtypeStruct((128, 1024), BF),
        ),
        in_specs=[pl.BlockSpec(memory_space=pl.ANY)] * 8,
        out_specs=(pl.BlockSpec(memory_space=pltpu.VMEM),) * 3,
        scratch_shapes=[
            vmem((K, 1024, 512), BF),
            vmem((2, K, 512, 512), BF),
            vmem((1024, 512), BF),
            vmem((512, 1024), BF),
            vmem((1024, 512), BF),
            vmem((1024, 512), BF),
            vmem((1024, 1024), BF),
            vmem((1024, 1024), BF),
            vmem((512, 1024), BF),
            vmem((1024, 512), F32),
            vmem((1024, 512), F32),
            vmem((1024, 512), BF),
            vmem((2, 4, 128, 1024), BF),
            vmem((4, 128, 1024), BF),
            vmem((3, 128, 1024), BF),
            vmem((3, 128, 1024), BF),
            vmem((1024, 1024), BF),
            vmem((1024, 512), BF),
            vmem((1024, 512), BF),
            vmem((K, 4, 512, 128), BF),
            vmem((K, 3, 512, 128), BF),
            vmem((K, 512, 128), BF),
            vmem((NZ, 512, 128), BF),
            vmem((3, 1024, 512), BF),
            vmem((3, 3, 256, 512), BF),
            vmem((3, 256, 512), BF),
            vmem((3, NZ, 32, 512), BF),
            vmem((2, 4, 256, 128), BF),
            vmem((2, NZ, 256, 128), BF),
            vmem((2, 256, 128), BF),
            vmem((2, NY, 32, 128), BF),
            dma((K + 3, 8)), dma((K + 3, 8)), dma((K,)), dma((K,)), dma((2,)),
            dma((K, 2)), dma((K, 4)), dma((2,)), dma((2,)), dma((2,)), dma((2, 2)), dma((2, 2)),
            dma((4,)), dma((4,)), dma((3,)), dma((3,)),
            dma((K, 3)), dma((K, 3)), dma((K,)), dma((NZ,)),
            dma((3, 3)), dma((3, 3)), dma((3, 4, 2)), dma((3, NZ)),
            dma((2, 4)), dma((2, NZ)), dma((2, NY, 2)), dma((2, NY)),
        ],
        compiler_params=pltpu.CompilerParams(
            collective_id=0, has_side_effects=True, vmem_limit_bytes=63 * 2**20
        ),
        name="backward",
    )(cotangent, features, normed, pre_hidden, pre_inner, w_first, w_second, w_down)
    grad_second, first, down_rows, grad_up, enc_rows = pl.pallas_call(
        functools.partial(finish, factor=factor),
        out_shape=(
            jax.ShapeDtypeStruct((512, 128), F32),
            jax.ShapeDtypeStruct((32, 512), F32),
            jax.ShapeDtypeStruct((32, 512), F32),
            jax.ShapeDtypeStruct((32, 512), F32),
            jax.ShapeDtypeStruct((128, 1024), BF),
        ),
        name="finish",
    )(gs, small, own_rows)
    return (grad_second, first, down_rows.T, grad_up, enc_rows)


def solution(mesh):
    return jax.shard_map(
        on_device,
        mesh=mesh,
        in_specs=(
            P(("dp", "tensor"), None),
            P(("dp", "tensor"), None),
            P(("dp", "tensor"), None),
            P("dp", "tensor"),
            P("dp", "tensor"),
            P(None, "tensor"),
            P("tensor", None),
            P("tensor", None),
        ),
        out_specs=(
            P("tensor", "dp"),
            P("dp", "tensor"),
            P("tensor", "dp"),
            P("dp", "tensor"),
            P(("dp", "tensor"), None),
        ),
        check_vma=False,
    )
```
